128 devices in a mesh: fsdp: 8 (over z, x_lo), tp: 16 (over x_hi, y, core).
Axes of the slice: x: 4 (x_hi: 2, x_lo: 2; x = x_hi * 2 + x_lo), y: 4, z: 4, core: 2. Of those that a mesh axis runs over, the one named last changes fastest.
Arguments:
- weight: bfloat16 [16384, 26624], P('fsdp', 'tp')
- adapter_down_factor: bfloat16 [16384, 64], P(('fsdp', 'tp')), may hold values from -6 to 6
- adapter_up_factor: bfloat16 [64, 26624], P('fsdp', 'tp'), may hold values from -0.75 to 0.75
- magnitude: float32 [26624], P('tp'), may hold values from 100 to 1000
- training_column_block: int32 [16, 13], replicated, may hold values from 0 to 207, as said below
Outputs:
- merged: bfloat16 [16384, 26624], P('fsdp', 'tp')
The draws below stay inside these ranges and needn't reach their ends.
Inputs may be any that keep to these rules, and one draw needn't show every extreme that they name: training_column_block lists every column block once. Owner r's s-th block is block p_s of training shard (r - q_s) mod the tp axis size, i.e. training_column_block[r, s] = ((r - q_s) mod tp) * 13 + p_s, where p is a permutation of the 13 local positions and q takes 13 distinct offsets; at most 1 block of one training shard go to one owner, and exactly 1 do for some pair.
All inputs are finite; a program needn't handle non-finite values.
Results may differ from the reference program's by a relative error of at most 0.005.
Values may be sent and summed in bfloat16 or wider, within the bound.
No kernel may reach another device: no remote copies, remote signals or barrier semaphores. Data moves between devices by JAX's collectives and lax.ppermute only.
A program may use at most 128 MiB of HBM per device.

```python
import math
import jax
import jax.numpy as jnp
from jax import lax

MODEL_WIDTH = 16384
HIDDEN_UNITS = 26624
ADAPTER_RANK = 64
BLOCK = 128
BPS = 13
NBLK = 208
QN = 13
N_FSDP = 8
N_TP = 16


def draw_weight(key, part):
    key = jax.random.fold_in(key, 11)
    base_key, column_key = jax.random.split(key, 2)
    row_pos = jnp.arange(MODEL_WIDTH, dtype=jnp.float32)[:, None] / MODEL_WIDTH
    column_exp = jax.random.uniform(column_key, (1, HIDDEN_UNITS), jnp.float32, 0.0, 1.0)
    base = jax.random.normal(base_key, (MODEL_WIDTH, HIDDEN_UNITS), jnp.float32)
    row_scale = 10.0 ** row_pos
    values = base * row_scale * 10.0 ** column_exp
    return values.astype(jnp.bfloat16)


def draw_training_column_block(key, part):
    key = jax.random.fold_in(key, 23)
    offset_key, position_key = jax.random.split(key)
    ranking = jax.random.permutation(offset_key, N_TP).astype(jnp.int32)
    values = jnp.arange(N_TP, dtype=jnp.int32)
    favoured = ((values == 1) | (values == N_TP - 1) | (values == N_TP // 2)).astype(jnp.int32)
    scores = ranking + N_TP * favoured
    top_scores, offsets = lax.top_k(scores, QN)
    offsets = offsets.astype(jnp.int32)
    positions = jax.random.permutation(position_key, BPS).astype(jnp.int32)
    owner = jnp.arange(N_TP, dtype=jnp.int32)[:, None]
    local = jnp.arange(BPS, dtype=jnp.int32)[None, :]
    shard = (owner - offsets[local % QN]) % N_TP
    return (shard * BPS + positions[local]).astype(jnp.int32)


def block_levels(rng, extent, cuts, low, high):
    factor_of = 1.0
    for axis_at, blocks in cuts:
        draws = jax.random.uniform(jax.random.fold_in(jax.random.fold_in(rng, 6), axis_at), (blocks,), jnp.float32, low / len(cuts), high / len(cuts))
        factor_of = factor_of * jnp.repeat(jnp.exp(draws), extent[axis_at] // blocks).reshape((-1,) + (1,) * (len(extent) - 1 - axis_at))
    return factor_of


def centred(key, dims, width, reach, pieces=(), kind=jnp.bfloat16):
    drawn = width * jax.random.normal(key, dims, jnp.float32)
    if pieces:
        drawn = drawn * block_levels(key, dims, pieces, -0.22, 0.18)
    return jnp.clip(drawn, -reach, reach).astype(kind)


def setup_inputs(seed: int = 0) -> dict:
    keys = jax.random.split(jax.random.key(seed), 6)
    return {
        "weight": draw_weight(jax.random.fold_in(keys[5], 71), 0),
        "adapter_down_factor": centred(keys[1], (MODEL_WIDTH, ADAPTER_RANK), 1.0, 6.0, ((0, 128),)),
        "adapter_up_factor": centred(keys[2], (ADAPTER_RANK, HIDDEN_UNITS), ADAPTER_RANK ** -0.5, 0.75, ((0, 8), (1, 16))),
        "magnitude": jnp.clip(jnp.exp(math.log(1000.0) - 2.3025851 * jax.random.uniform(keys[3], (HIDDEN_UNITS,), jnp.float32) ** block_levels(keys[3], (HIDDEN_UNITS,), ((0, 16),), -0.2, 0.2)), 100.0, 1000.0),
        "training_column_block": draw_training_column_block(jax.random.fold_in(keys[5], 71), 0),
    }


def reference(weight, adapter_down_factor, adapter_up_factor, magnitude, training_column_block):
    weight_slabs = weight.reshape(N_FSDP, MODEL_WIDTH // N_FSDP, HIDDEN_UNITS)
    adapter_tiles = adapter_down_factor.reshape(N_FSDP, MODEL_WIDTH // N_FSDP, ADAPTER_RANK)

    def combine_rows(pair):
        weight_part, adapter_piece = pair
        low_rank_update = jnp.dot(adapter_piece, adapter_up_factor, preferred_element_type=jnp.float32)
        return (weight_part.astype(jnp.float32) + low_rank_update).astype(jnp.bfloat16)
    combined = lax.map(combine_rows, (weight_slabs, adapter_tiles))

    def square_sums(part):
        return lax.optimization_barrier(jnp.sum(jnp.square(part.astype(jnp.float32)), axis=0))
    squares = lax.optimization_barrier(jnp.sum(lax.map(square_sums, combined), axis=0))
    col_scale = magnitude * lax.rsqrt(squares + 1e-06)

    def apply_scale(part):
        return (part.astype(jnp.float32) * col_scale[None, :]).astype(jnp.bfloat16)
    scaled = lax.map(apply_scale, combined).reshape(MODEL_WIDTH, NBLK, BLOCK)
    merged = jnp.take(scaled, training_column_block.reshape(-1).astype(jnp.int32), axis=1)
    return merged.reshape(MODEL_WIDTH, HIDDEN_UNITS)
```

```python
import functools

import jax
import jax.numpy as jnp
from jax import lax
from jax.experimental import pallas as pl
from jax.experimental.pallas import tpu as pltpu
from jax.sharding import PartitionSpec as P

AXES = ("fsdp", "tp")
BLK = 128
SCALE_ROWS = 16
EXTRA = 80
OWN = (0, 0)
A_MASKS = (2, 6, 8, 1)
B_MASKS = (1, 2, 6)
BF16, F32 = jnp.bfloat16, jnp.float32
HBM = pl.BlockSpec(memory_space=pltpu.HBM)
ANY = pl.BlockSpec(memory_space=pl.ANY)
SMEM = pl.BlockSpec(memory_space=pltpu.SMEM)
VMEM = pl.BlockSpec(memory_space=pltpu.VMEM)


def shift_to(t, offset, flip):
    hi, y, core = t // 8, (t // 2) % 4, t % 2
    return ((hi + offset[0]) % 2) * 8 + ((y + offset[1]) % 4) * 2 + (core + flip) % 2


def tp_perm(offset, flip=0):
    return [(f * 16 + t, f * 16 + shift_to(t, offset, flip)) for f in range(8) for t in range(16)]


def tp_xor(mask):
    return [(f * 16 + t, f * 16 + (t ^ mask)) for f in range(8) for t in range(16)]


def fsdp_xor(mask):
    return [(f * 16 + t, (f ^ mask) * 16 + t) for f in range(8) for t in range(16)]


def send(x, perm):
    return lax.ppermute(x, AXES, perm)


def fill_tables(tcb, t, block_to, column_from):
    for i in range(16):
        block_to[i] = 0
        column_from[i] = -1
    for s in range(tcb.shape[1]):
        value = tcb[0, s]
        shard = value // tcb.shape[1]
        shift = (16 - shard) % 16
        block_to[(t + shift) % 16] = value - shard * tcb.shape[1]
        column_from[(t + 16 - shift) % 16] = s


def params(limit_mib, **kw):
    return pltpu.CompilerParams(vmem_limit_bytes=limit_mib << 20, **kw)


def columns(j):
    return pl.ds(pl.multiple_of(j * BLK, BLK), BLK)


def both(offset):
    return ((offset, 0), (offset, 1))


def pack_kernel(messages, tcb, w, *refs):
    outs, (buf, block_to, column_from, in_sems, out_sems) = refs[: len(messages)], refs[len(messages) :]
    t = lax.axis_index("tp")
    fill_tables(tcb, t, block_to, column_from)
    copies = []
    for out, message in zip(outs, messages):
        for n, (offset, flip) in enumerate(message):
            i, j = len(copies), block_to[shift_to(t, offset, flip)]
            copies.append(
                (
                    pltpu.make_async_copy(w.at[:, columns(j)], buf.at[i], in_sems.at[i]),
                    pltpu.make_async_copy(buf.at[i], out.at[n], out_sems.at[i]),
                )
            )
    for fetch, _ in copies:
        fetch.start()
    for fetch, store in copies:
        fetch.wait()
        store.start()
    for _, store in copies:
        store.wait()


def pack(tcb, w, messages):
    rows, count = w.shape[0], sum(len(m) for m in messages)
    return pl.pallas_call(
        functools.partial(pack_kernel, messages),
        out_shape=[jax.ShapeDtypeStruct((len(m), rows, BLK), BF16) for m in messages],
        in_specs=[SMEM, HBM],
        out_specs=[HBM] * len(messages),
        scratch_shapes=[
            pltpu.VMEM((count, rows, BLK), BF16),
            pltpu.SMEM((16,), jnp.int32),
            pltpu.SMEM((16,), jnp.int32),
            pltpu.SemaphoreType.DMA((count,)),
            pltpu.SemaphoreType.DMA((count,)),
        ],
        compiler_params=params(60),
        cost_estimate=pl.CostEstimate(flops=0, bytes_accessed=count * 4 * rows * BLK, transcendentals=0),
        name="pack",
    )(tcb, w)


def squares_kernel(w_hbm, a_rel, b_rel, sq, a_ord, b_ord, w, sems):
    t, f = lax.axis_index("tp"), lax.axis_index("fsdp")
    count, tile, width = w.shape
    fetches = [
        pltpu.make_async_copy(w_hbm.at[pl.ds(i * tile, tile)], w.at[i], sems.at[i]) for i in range(count)
    ]
    for c in fetches:
        c.start()
    row = lax.broadcasted_iota(jnp.int32, (64, 64), 0)
    col = lax.broadcasted_iota(jnp.int32, (64, 64), 1)
    slot = col >> 3
    shard = (slot ^ ((slot >> 1) & 2)) ^ f
    place = jnp.where(row == shard * 8 + (col & 7), 1.0, 0.0).astype(BF16)
    b_ord[...] = jnp.dot(place, b_rel[...], preferred_element_type=F32).astype(BF16)
    for i in range(16):
        rel = i ^ t
        r0, r1, r2, r3 = rel & 1, (rel >> 1) & 1, (rel >> 2) & 1, (rel >> 3) & 1
        slot = (r1 ^ r2) | (r2 << 1) | (r3 << 2) | (r0 << 3)
        a_ord[i * 128 : (i + 1) * 128, :] = a_rel[:, columns(slot)].astype(F32).T.astype(BF16)
    sums = [jnp.zeros((8, min(256, width - lo)), F32) for lo in range(0, width, 256)]
    for i in range(count):
        fetches[i].wait()
        a = a_ord[i * tile : (i + 1) * tile, :]
        for n, lo in enumerate(range(0, width, 256)):
            hi = min(lo + 256, width)
            low_rank = jnp.dot(a, b_ord[:, lo:hi], preferred_element_type=F32)
            combined = (w[i, :, lo:hi].astype(F32) + low_rank).astype(BF16).astype(F32)
            sums[n] += jnp.sum((combined * combined).reshape(tile // 8, 8, hi - lo), axis=0)
    for n, lo in enumerate(range(0, width, 256)):
        sq[:, lo : min(lo + 256, width)] = jnp.sum(sums[n], axis=0, keepdims=True)


def squares(w, a_rel, b_rel, tile=256):
    rows, width = w.shape
    return pl.pallas_call(
        squares_kernel,
        out_shape=[
            jax.ShapeDtypeStruct((1, width), F32),
            jax.ShapeDtypeStruct((rows, 64), BF16),
            jax.ShapeDtypeStruct((64, width), BF16),
        ],
        in_specs=[HBM, VMEM, VMEM],
        out_specs=[VMEM] * 3,
        scratch_shapes=[
            pltpu.VMEM((rows // tile, tile, width), BF16),
            pltpu.SemaphoreType.DMA((rows // tile,)),
        ],
        compiler_params=params(60),
        cost_estimate=pl.CostEstimate(flops=2 * rows * width * 64, bytes_accessed=2 * rows * width, transcendentals=0),
        name="column_squares",
    )(w, a_rel, b_rel)


def extras_kernel(tcb, b, sq, mag, out, buf, block_to, column_from, sems):
    fill_tables(tcb, lax.axis_index("tp"), block_to, column_from)
    scale = mag[...] * lax.rsqrt(sq[...] + 1e-06)
    row = lax.broadcasted_iota(jnp.int32, (SCALE_ROWS, BLK), 0)
    for j in range(buf.shape[0]):
        cols = slice(j * BLK, (j + 1) * BLK)
        s = scale[:, cols]
        high = s.astype(BF16).astype(F32)
        mid = (s - high).astype(BF16).astype(F32)
        low = s - high - mid
        parts = jnp.where(row == 0, high, jnp.where(row == 1, mid, jnp.where(row == 2, low, 0.0)))
        buf[j, 0:SCALE_ROWS, :] = parts.astype(BF16)
        buf[j, SCALE_ROWS:EXTRA, :] = b[:, cols]
    copies = [pltpu.make_async_copy(buf.at[block_to[r]], out.at[r], sems.at[r]) for r in range(16)]
    for c in copies:
        c.start()
    for c in copies:
        c.wait()


def pack_extras(tcb, b, sq, mag):
    per_shard = tcb.shape[1]
    return pl.pallas_call(
        extras_kernel,
        out_shape=jax.ShapeDtypeStruct((16, EXTRA, BLK), BF16),
        in_specs=[SMEM, VMEM, VMEM, VMEM],
        out_specs=HBM,
        scratch_shapes=[
            pltpu.VMEM((per_shard, EXTRA, BLK), BF16),
            pltpu.SMEM((16,), jnp.int32),
            pltpu.SMEM((16,), jnp.int32),
            pltpu.SemaphoreType.DMA((16,)),
        ],
        compiler_params=params(60),
        name="pack_extras",
    )(tcb, b, sq, mag)


def finish_kernel(blocks, first, tcb, a, extras, *refs):
    n = len(blocks)
    arrived, refs = refs[:n], refs[n if first else n + 1 :]
    out, raw, extra, done, block_to, column_from, raw_sems, extra_sems, done_sems = refs
    t = lax.axis_index("tp")
    fill_tables(tcb, t, block_to, column_from)
    here, fetches, stores = [], [], []
    for u, ((dx, dy), flip, at) in enumerate(blocks):
        shard = shift_to(t, (dx, (4 - dy) % 4), flip)
        column = column_from[shard]
        here.append(column >= 0)
        fetches.append(
            (
                pltpu.make_async_copy(extras.at[shard], extra.at[u], extra_sems.at[u]),
                pltpu.make_async_copy(arrived[u].at[at], raw.at[u], raw_sems.at[u]),
            )
        )
        target = out.at[:, columns(jnp.maximum(column, 0))]
        stores.append(pltpu.make_async_copy(done.at[u], target, done_sems.at[u]))
    for pair in fetches:
        for c in pair:
            c.start()
    for u in range(n):
        for c in fetches[u]:
            c.wait()

        @pl.when(here[u])
        def _():
            parts = extra[u, 0:SCALE_ROWS, :].astype(F32)
            scale = parts[0:1] + parts[1:2] + parts[2:3]
            b = extra[u, SCALE_ROWS:EXTRA, :]
            for lo in range(0, a.shape[0], 256):
                rows = slice(lo, lo + 256)
                low_rank = jnp.dot(a[rows, :], b, preferred_element_type=F32)
                combined = (raw[u, rows, :].astype(F32) + low_rank).astype(BF16).astype(F32)
                done[u, rows, :] = (combined * scale).astype(BF16)
            stores[u].start()

    for u in range(n):
        pl.when(here[u])(stores[u].wait)


def finish(tcb, a, extras, blocks, merged=None, width=None):
    rows, n, first = a.shape[0], len(blocks), merged is None
    arrays = [block[2] for block in blocks] + ([] if first else [merged])
    width = width if first else merged.shape[1]
    return pl.pallas_call(
        functools.partial(finish_kernel, [(block[0], block[1], block[3]) for block in blocks], first),
        out_shape=jax.ShapeDtypeStruct((rows, width), BF16),
        in_specs=[SMEM, VMEM, HBM] + [HBM] * len(arrays),
        out_specs=HBM,
        input_output_aliases={} if first else {3 + n: 0},
        scratch_shapes=[
            pltpu.VMEM((n, rows, BLK), BF16),
            pltpu.VMEM((n, EXTRA, BLK), BF16),
            pltpu.VMEM((n, rows, BLK), BF16),
            pltpu.SMEM((16,), jnp.int32),
            pltpu.SMEM((16,), jnp.int32),
            pltpu.SemaphoreType.DMA((n,)),
            pltpu.SemaphoreType.DMA((n,)),
            pltpu.SemaphoreType.DMA((n,)),
        ],
        compiler_params=params(60),
        cost_estimate=pl.CostEstimate(
            flops=2 * n * rows * BLK * 64, bytes_accessed=4 * n * rows * BLK, transcendentals=0
        ),
        name="finish",
    )(tcb, a, extras, *arrays)


def per_device(weight, adapter_down_factor, adapter_up_factor, magnitude, training_column_block):
    tcb = training_column_block
    after = lax.optimization_barrier
    chips = ((1, 0), (0, 1), (0, 3), (1, 2))
    singles = [(o, flip) for flip in range(2) for o in ((1, 1), (1, 3), (0, 2))]
    head = list(pack(tcb, weight, [both(o) for o in chips[:3]]))
    a, b = adapter_down_factor.T, adapter_up_factor
    a = jnp.concatenate([a, send(a, tp_xor(A_MASKS[0]))], axis=1)
    b = jnp.concatenate([b, send(b, fsdp_xor(B_MASKS[0]))], axis=0)
    a, b, head = after((a, b, head))
    direct = [None] * 4
    for n in (1, 2):
        direct[n] = send(head[n], tp_perm(chips[n]))
    for mask in A_MASKS[1:3]:
        a = jnp.concatenate([a, send(a, tp_xor(mask))], axis=1)
    a, head[0], weight_then = after((a, head[0], weight))
    direct[0] = send(head[0], tp_perm(chips[0]))
    a = jnp.concatenate([a, send(a, tp_xor(A_MASKS[3]))], axis=1)
    for mask in B_MASKS[1:]:
        b = jnp.concatenate([b, send(b, fsdp_xor(mask))], axis=0)
    sq, a, b = squares(weight, a, b)
    fourth, own, *single = pack(tcb, weight_then, [both(chips[3]), both(OWN)] + [(x,) for x in singles])
    sq = sq + send(sq, fsdp_xor(1))
    sq, direct[:3], fourth = after((sq, direct[:3], fourth))
    direct[3] = send(fourth, tp_perm(chips[3]))
    for mask in (2, 6):
        sq = sq + send(sq, fsdp_xor(mask))
    extras = pack_extras(tcb, b, sq, magnitude[None, :])
    extras = lax.all_to_all(extras, "tp", split_axis=0, concat_axis=0, tiled=True)
    extras, direct[3], single, own = after((extras, direct[3], single, own))
    single = [send(m, tp_perm(*x)) for m, x in zip(single, singles)]
    blocks = [(OWN, 0, own, 0), (OWN, 1, send(own, tp_xor(1)), 1)]
    for o, m in zip(chips, direct):
        blocks += [(o, 0, m, 0), (o, 1, send(m, tp_xor(1)), 1)]
    merged = finish(tcb, a, extras, blocks, width=weight.shape[1])
    merged = finish(tcb, a, extras, [(*x, m, 0) for x, m in zip(singles[:3], single[:3])], merged)
    return finish(tcb, a, extras, [(*x, m, 0) for x, m in zip(singles[3:], single[3:])], merged)


def solution(mesh):
    return jax.shard_map(
        per_device,
        mesh=mesh,
        in_specs=(P("fsdp", "tp"), P(("fsdp", "tp"), None), P("fsdp", "tp"), P("tp"), P()),
        out_specs=P("fsdp", "tp"),
        check_vma=False,
    )
```

```python
import functools

import jax
import jax.numpy as jnp
from jax import lax
from jax.experimental import pallas as pl
from jax.experimental.pallas import tpu as pltpu
from jax.sharding import PartitionSpec as P

AXES = ("fsdp", "tp")
BLK = 128
SCALE_ROWS = 16
EXTRA = 80
OWN = (0, 0)
A_MASKS = (2, 6, 8, 1)
B_MASKS = (1, 2, 6)
BF16, F32 = jnp.bfloat16, jnp.float32
HBM = pl.BlockSpec(memory_space=pltpu.HBM)
ANY = pl.BlockSpec(memory_space=pl.ANY)
SMEM = pl.BlockSpec(memory_space=pltpu.SMEM)
VMEM = pl.BlockSpec(memory_space=pltpu.VMEM)


def shift_to(t, offset, flip):
    hi, y, core = t // 8, (t // 2) % 4, t % 2
    return ((hi + offset[0]) % 2) * 8 + ((y + offset[1]) % 4) * 2 + (core + flip) % 2


def tp_perm(offset, flip=0):
    return [(f * 16 + t, f * 16 + shift_to(t, offset, flip)) for f in range(8) for t in range(16)]


def tp_xor(mask):
    return [(f * 16 + t, f * 16 + (t ^ mask)) for f in range(8) for t in range(16)]


def fsdp_xor(mask):
    return [(f * 16 + t, (f ^ mask) * 16 + t) for f in range(8) for t in range(16)]


def send(x, perm):
    return lax.ppermute(x, AXES, perm)


def fill_tables(tcb, t, block_to, column_from):
    for i in range(16):
        block_to[i] = 0
        column_from[i] = -1
    for s in range(tcb.shape[1]):
        value = tcb[0, s]
        shard = value // tcb.shape[1]
        shift = (16 - shard) % 16
        block_to[(t + shift) % 16] = value - shard * tcb.shape[1]
        column_from[(t + 16 - shift) % 16] = s


def params(limit_mib, **kw):
    return pltpu.CompilerParams(vmem_limit_bytes=limit_mib << 20, **kw)


def columns(j):
    return pl.ds(pl.multiple_of(j * BLK, BLK), BLK)


def both(offset):
    return ((offset, 0), (offset, 1))


def pack_kernel(messages, tcb, w, *refs):
    outs, (buf, block_to, column_from, in_sems, out_sems) = refs[: len(messages)], refs[len(messages) :]
    t = lax.axis_index("tp")
    fill_tables(tcb, t, block_to, column_from)
    copies = []
    for out, message in zip(outs, messages):
        for n, (offset, flip) in enumerate(message):
            i, j = len(copies), block_to[shift_to(t, offset, flip)]
            copies.append(
                (
                    pltpu.make_async_copy(w.at[:, columns(j)], buf.at[i], in_sems.at[i]),
                    pltpu.make_async_copy(buf.at[i], out.at[n], out_sems.at[i]),
                )
            )
    for fetch, _ in copies:
        fetch.start()
    for fetch, store in copies:
        fetch.wait()
        store.start()
    for _, store in copies:
        store.wait()


def pack(tcb, w, messages):
    rows, count = w.shape[0], sum(len(m) for m in messages)
    return pl.pallas_call(
        functools.partial(pack_kernel, messages),
        out_shape=[jax.ShapeDtypeStruct((len(m), rows, BLK), BF16) for m in messages],
        in_specs=[SMEM, HBM],
        out_specs=[HBM] * len(messages),
        scratch_shapes=[
            pltpu.VMEM((count, rows, BLK), BF16),
            pltpu.SMEM((16,), jnp.int32),
            pltpu.SMEM((16,), jnp.int32),
            pltpu.SemaphoreType.DMA((count,)),
            pltpu.SemaphoreType.DMA((count,)),
        ],
        compiler_params=params(60),
        cost_estimate=pl.CostEstimate(flops=0, bytes_accessed=count * 4 * rows * BLK, transcendentals=0),
        name="pack",
    )(tcb, w)


def squares_kernel(w_hbm, a_rel, b_rel, sq, a_ord, b_ord, w, sems):
    t, f = lax.axis_index("tp"), lax.axis_index("fsdp")
    count, tile, width = w.shape
    fetches = [
        pltpu.make_async_copy(w_hbm.at[pl.ds(i * tile, tile)], w.at[i], sems.at[i]) for i in range(count)
    ]
    for c in fetches:
        c.start()
    row = lax.broadcasted_iota(jnp.int32, (64, 64), 0)
    col = lax.broadcasted_iota(jnp.int32, (64, 64), 1)
    slot = col >> 3
    shard = (slot ^ ((slot >> 1) & 2)) ^ f
    place = jnp.where(row == shard * 8 + (col & 7), 1.0, 0.0).astype(BF16)
    b_ord[...] = jnp.dot(place, b_rel[...], preferred_element_type=F32).astype(BF16)
    for i in range(16):
        rel = i ^ t
        r0, r1, r2, r3 = rel & 1, (rel >> 1) & 1, (rel >> 2) & 1, (rel >> 3) & 1
        slot = (r1 ^ r2) | (r2 << 1) | (r3 << 2) | (r0 << 3)
        a_ord[i * 128 : (i + 1) * 128, :] = a_rel[:, columns(slot)].astype(F32).T.astype(BF16)
    sums = [jnp.zeros((8, min(256, width - lo)), F32) for lo in range(0, width, 256)]
    for i in range(count):
        fetches[i].wait()
        a = a_ord[i * tile : (i + 1) * tile, :]
        for n, lo in enumerate(range(0, width, 256)):
            hi = min(lo + 256, width)
            low_rank = jnp.dot(a, b_ord[:, lo:hi], preferred_element_type=F32)
            combined = (w[i, :, lo:hi].astype(F32) + low_rank).astype(BF16).astype(F32)
            sums[n] += jnp.sum((combined * combined).reshape(tile // 8, 8, hi - lo), axis=0)
    for n, lo in enumerate(range(0, width, 256)):
        sq[:, lo : min(lo + 256, width)] = jnp.sum(sums[n], axis=0, keepdims=True)


def squares(w, a_rel, b_rel, tile=256):
    rows, width = w.shape
    return pl.pallas_call(
        squares_kernel,
        out_shape=[
            jax.ShapeDtypeStruct((1, width), F32),
            jax.ShapeDtypeStruct((rows, 64), BF16),
            jax.ShapeDtypeStruct((64, width), BF16),
        ],
        in_specs=[HBM, VMEM, VMEM],
        out_specs=[VMEM] * 3,
        scratch_shapes=[
            pltpu.VMEM((rows // tile, tile, width), BF16),
            pltpu.SemaphoreType.DMA((rows // tile,)),
        ],
        compiler_params=params(60),
        cost_estimate=pl.CostEstimate(flops=2 * rows * width * 64, bytes_accessed=2 * rows * width, transcendentals=0),
        name="column_squares",
    )(w, a_rel, b_rel)


def extras_kernel(tcb, b, sq, mag, out, buf, block_to, column_from, sems):
    fill_tables(tcb, lax.axis_index("tp"), block_to, column_from)
    scale = mag[...] * lax.rsqrt(sq[...] + 1e-06)
    row = lax.broadcasted_iota(jnp.int32, (SCALE_ROWS, BLK), 0)
    for j in range(buf.shape[0]):
        cols = slice(j * BLK, (j + 1) * BLK)
        s = scale[:, cols]
        high = s.astype(BF16).astype(F32)
        mid = (s - high).astype(BF16).astype(F32)
        low = s - high - mid
        parts = jnp.where(row == 0, high, jnp.where(row == 1, mid, jnp.where(row == 2, low, 0.0)))
        buf[j, 0:SCALE_ROWS, :] = parts.astype(BF16)
        buf[j, SCALE_ROWS:EXTRA, :] = b[:, cols]
    copies = [pltpu.make_async_copy(buf.at[block_to[r]], out.at[r], sems.at[r]) for r in range(16)]
    for c in copies:
        c.start()
    for c in copies:
        c.wait()


def pack_extras(tcb, b, sq, mag):
    per_shard = tcb.shape[1]
    return pl.pallas_call(
        extras_kernel,
        out_shape=jax.ShapeDtypeStruct((16, EXTRA, BLK), BF16),
        in_specs=[SMEM, VMEM, VMEM, VMEM],
        out_specs=HBM,
        scratch_shapes=[
            pltpu.VMEM((per_shard, EXTRA, BLK), BF16),
            pltpu.SMEM((16,), jnp.int32),
            pltpu.SMEM((16,), jnp.int32),
            pltpu.SemaphoreType.DMA((16,)),
        ],
        compiler_params=params(60),
        name="pack_extras",
    )(tcb, b, sq, mag)


def finish_kernel(blocks, first, near, tcb, a, extras, *refs):
    n = len(blocks)
    arrived, refs = refs[:n], refs[n if first else n + 1 :]
    out, raw, extra, done, block_to, column_from, raw_sems, extra_sems, done_sems = refs
    t = lax.axis_index("tp")
    fill_tables(tcb, t, block_to, column_from)
    here, fetches, stores = [], [], []
    for u, ((dx, dy), flip, at) in enumerate(blocks):
        shard = shift_to(t, (dx, (4 - dy) % 4), flip)
        column = column_from[shard]
        here.append(column >= 0)
        fetches.append([pltpu.make_async_copy(extras.at[shard], extra.at[u], extra_sems.at[u])])
        if not near:
            fetches[u].append(pltpu.make_async_copy(arrived[u].at[at], raw.at[u], raw_sems.at[u]))
        target = out.at[:, columns(jnp.maximum(column, 0))]
        stores.append(pltpu.make_async_copy(done.at[u], target, done_sems.at[u]))
    for pair in fetches:
        for c in pair:
            c.start()
    for u in range(n):
        for c in fetches[u]:
            c.wait()

        @pl.when(here[u])
        def _():
            parts = extra[u, 0:SCALE_ROWS, :].astype(F32)
            scale = parts[0:1] + parts[1:2] + parts[2:3]
            b = extra[u, SCALE_ROWS:EXTRA, :]
            block = arrived[u].at[blocks[u][2]] if near else raw.at[u]
            for lo in range(0, a.shape[0], 256):
                rows = slice(lo, lo + 256)
                low_rank = jnp.dot(a[rows, :], b, preferred_element_type=F32)
                combined = (block[rows, :].astype(F32) + low_rank).astype(BF16).astype(F32)
                done[u, rows, :] = (combined * scale).astype(BF16)
            stores[u].start()

    for u in range(n):
        pl.when(here[u])(stores[u].wait)


def finish(tcb, a, extras, blocks, merged=None, width=None, near=False):
    rows, n, first = a.shape[0], len(blocks), merged is None
    arrays = [block[2] for block in blocks] + ([] if first else [merged])
    width = width if first else merged.shape[1]
    return pl.pallas_call(
        functools.partial(finish_kernel, [(block[0], block[1], block[3]) for block in blocks], first, near),
        out_shape=jax.ShapeDtypeStruct((rows, width), BF16),
        in_specs=[SMEM, VMEM, HBM] + [VMEM if near else HBM] * n + [HBM] * (len(arrays) - n),
        out_specs=HBM,
        input_output_aliases={} if first else {3 + n: 0},
        scratch_shapes=[
            pltpu.VMEM((1 if near else n, rows, BLK), BF16),
            pltpu.VMEM((n, EXTRA, BLK), BF16),
            pltpu.VMEM((n, rows, BLK), BF16),
            pltpu.SMEM((16,), jnp.int32),
            pltpu.SMEM((16,), jnp.int32),
            pltpu.SemaphoreType.DMA((n,)),
            pltpu.SemaphoreType.DMA((n,)),
            pltpu.SemaphoreType.DMA((n,)),
        ],
        compiler_params=params(12 if near else 60),
        cost_estimate=pl.CostEstimate(
            flops=2 * n * rows * BLK * 64, bytes_accessed=4 * n * rows * BLK, transcendentals=0
        ),
        name="finish",
    )(tcb, a, extras, *arrays)


def per_device(weight, adapter_down_factor, adapter_up_factor, magnitude, training_column_block):
    tcb = training_column_block
    after = lax.optimization_barrier
    chips = ((1, 0), (0, 1), (0, 3), (1, 2))
    singles = [(o, flip) for flip in range(2) for o in ((1, 1), (1, 3), (0, 2))]
    head = list(pack(tcb, weight, [both(o) for o in chips[:3]]))
    a, b = adapter_down_factor.T, adapter_up_factor
    a = jnp.concatenate([a, send(a, tp_xor(A_MASKS[0]))], axis=1)
    b = jnp.concatenate([b, send(b, fsdp_xor(B_MASKS[0]))], axis=0)
    a, b, head = after((a, b, head))
    direct = [None] * 4
    for n in (1, 2):
        direct[n] = send(head[n], tp_perm(chips[n]))
    for mask in A_MASKS[1:3]:
        a = jnp.concatenate([a, send(a, tp_xor(mask))], axis=1)
    a, head[0], weight_then = after((a, head[0], weight))
    direct[0] = send(head[0], tp_perm(chips[0]))
    a = jnp.concatenate([a, send(a, tp_xor(A_MASKS[3]))], axis=1)
    for mask in B_MASKS[1:]:
        b = jnp.concatenate([b, send(b, fsdp_xor(mask))], axis=0)
    sq, a, b = squares(weight, a, b)
    fourth, own = pack(tcb, weight_then, [both(chips[3]), both(OWN)])
    sq = sq + send(sq, fsdp_xor(1))
    sq, direct[:3], fourth = after((sq, direct[:3], fourth))
    direct[3] = send(fourth, tp_perm(chips[3]))
    for mask in (2, 6):
        sq = sq + send(sq, fsdp_xor(mask))
    extras = pack_extras(tcb, b, sq, magnitude[None, :])
    extras, weight_then = after((extras, weight))
    single = list(pack(tcb, weight_then, [(x,) for x in singles]))
    extras = lax.all_to_all(extras, "tp", split_axis=0, concat_axis=0, tiled=True)
    extras, direct[3], single, own = after((extras, direct[3], single, own))
    single = [send(m, tp_perm(*x)) for m, x in zip(single, singles)]
    blocks = [(OWN, 0, own, 0), (OWN, 1, send(own, tp_xor(1)), 1)]
    for o, m in zip(chips, direct):
        blocks += [(o, 0, m, 0), (o, 1, send(m, tp_xor(1)), 1)]
    blocks += [(*x, m, 0) for x, m in zip(singles, single)]
    merged = finish(tcb, a, extras, blocks[:10], width=weight.shape[1])
    merged = finish(tcb, a, extras, blocks[10:13], merged)
    return finish(tcb, a, extras, blocks[13:], merged, near=True)


def solution(mesh):
    return jax.shard_map(
        per_device,
        mesh=mesh,
        in_specs=(P("fsdp", "tp"), P(("fsdp", "tp"), None), P("fsdp", "tp"), P("tp"), P()),
        out_specs=P("fsdp", "tp"),
        check_vma=False,
    )
```

```python
import functools

import jax
import jax.numpy as jnp
from jax import lax
from jax.experimental import pallas as pl
from jax.experimental.pallas import tpu as pltpu
from jax.sharding import PartitionSpec as P

AXES = ("fsdp", "tp")
BLK = 128
SCALE_ROWS = 16
EXTRA = 80
OWN = (0, 0)
A_MASKS = (8, 2, 6, 1)
B_MASKS = (1, 2, 6)
BF16, F32 = jnp.bfloat16, jnp.float32
HBM = pl.BlockSpec(memory_space=pltpu.HBM)
ANY = pl.BlockSpec(memory_space=pl.ANY)
SMEM = pl.BlockSpec(memory_space=pltpu.SMEM)
VMEM = pl.BlockSpec(memory_space=pltpu.VMEM)


def shift_to(t, offset, flip):
    hi, y, core = t // 8, (t // 2) % 4, t % 2
    return ((hi + offset[0]) % 2) * 8 + ((y + offset[1]) % 4) * 2 + (core + flip) % 2


def tp_perm(offset, flip=0):
    return [(f * 16 + t, f * 16 + shift_to(t, offset, flip)) for f in range(8) for t in range(16)]


def tp_xor(mask):
    return [(f * 16 + t, f * 16 + (t ^ mask)) for f in range(8) for t in range(16)]


def fsdp_xor(mask):
    return [(f * 16 + t, (f ^ mask) * 16 + t) for f in range(8) for t in range(16)]


def send(x, perm):
    return lax.ppermute(x, AXES, perm)


def fill_tables(tcb, t, block_to, column_from):
    for i in range(16):
        block_to[i] = 0
        column_from[i] = -1
    for s in range(tcb.shape[1]):
        value = tcb[0, s]
        shard = value // tcb.shape[1]
        shift = (16 - shard) % 16
        block_to[(t + shift) % 16] = value - shard * tcb.shape[1]
        column_from[(t + 16 - shift) % 16] = s


def params(limit_mib, **kw):
    return pltpu.CompilerParams(vmem_limit_bytes=limit_mib << 20, **kw)


def columns(j):
    return pl.ds(pl.multiple_of(j * BLK, BLK), BLK)


def both(offset):
    return ((offset, 0), (offset, 1))


def pack_kernel(messages, tcb, w, *refs):
    outs, (buf, block_to, column_from, in_sems, out_sems) = refs[: len(messages)], refs[len(messages) :]
    t = lax.axis_index("tp")
    fill_tables(tcb, t, block_to, column_from)
    copies = []
    for out, message in zip(outs, messages):
        for n, (offset, flip) in enumerate(message):
            i, j = len(copies), block_to[shift_to(t, offset, flip)]
            copies.append(
                (
                    pltpu.make_async_copy(w.at[:, columns(j)], buf.at[i], in_sems.at[i]),
                    pltpu.make_async_copy(buf.at[i], out.at[n], out_sems.at[i]),
                )
            )
    for fetch, _ in copies:
        fetch.start()
    for fetch, store in copies:
        fetch.wait()
        store.start()
    for _, store in copies:
        store.wait()


def pack(tcb, w, messages):
    rows, count = w.shape[0], sum(len(m) for m in messages)
    return pl.pallas_call(
        functools.partial(pack_kernel, messages),
        out_shape=[jax.ShapeDtypeStruct((len(m), rows, BLK), BF16) for m in messages],
        in_specs=[SMEM, HBM],
        out_specs=[HBM] * len(messages),
        scratch_shapes=[
            pltpu.VMEM((count, rows, BLK), BF16),
            pltpu.SMEM((16,), jnp.int32),
            pltpu.SMEM((16,), jnp.int32),
            pltpu.SemaphoreType.DMA((count,)),
            pltpu.SemaphoreType.DMA((count,)),
        ],
        compiler_params=params(60),
        cost_estimate=pl.CostEstimate(flops=0, bytes_accessed=count * 4 * rows * BLK, transcendentals=0),
        name="pack",
    )(tcb, w)


def squares_kernel(w_hbm, a_rel, b_rel, sq, a_ord, b_ord, w, sems):
    t, f = lax.axis_index("tp"), lax.axis_index("fsdp")
    count, tile, width = w.shape
    fetches = [
        pltpu.make_async_copy(w_hbm.at[pl.ds(i * tile, tile)], w.at[i], sems.at[i]) for i in range(count)
    ]
    for c in fetches:
        c.start()
    row = lax.broadcasted_iota(jnp.int32, (64, 64), 0)
    col = lax.broadcasted_iota(jnp.int32, (64, 64), 1)
    slot = col >> 3
    shard = (slot ^ ((slot >> 1) & 2)) ^ f
    place = jnp.where(row == shard * 8 + (col & 7), 1.0, 0.0).astype(BF16)
    b_ord[...] = jnp.dot(place, b_rel[...], preferred_element_type=F32).astype(BF16)
    for i in range(16):
        rel = i ^ t
        r0, r1, r2, r3 = rel & 1, (rel >> 1) & 1, (rel >> 2) & 1, (rel >> 3) & 1
        slot = r3 | ((r1 ^ r2) << 1) | (r2 << 2) | (r0 << 3)
        a_ord[i * 128 : (i + 1) * 128, :] = a_rel[:, columns(slot)].astype(F32).T.astype(BF16)
    sums = [jnp.zeros((8, min(256, width - lo)), F32) for lo in range(0, width, 256)]
    for i in range(count):
        fetches[i].wait()
        a = a_ord[i * tile : (i + 1) * tile, :]
        for n, lo in enumerate(range(0, width, 256)):
            hi = min(lo + 256, width)
            low_rank = jnp.dot(a, b_ord[:, lo:hi], preferred_element_type=F32)
            combined = (w[i, :, lo:hi].astype(F32) + low_rank).astype(BF16).astype(F32)
            sums[n] += jnp.sum((combined * combined).reshape(tile // 8, 8, hi - lo), axis=0)
    for n, lo in enumerate(range(0, width, 256)):
        sq[:, lo : min(lo + 256, width)] = jnp.sum(sums[n], axis=0, keepdims=True)


def squares(w, a_rel, b_rel, tile=256):
    rows, width = w.shape
    return pl.pallas_call(
        squares_kernel,
        out_shape=[
            jax.ShapeDtypeStruct((1, width), F32),
            jax.ShapeDtypeStruct((rows, 64), BF16),
            jax.ShapeDtypeStruct((64, width), BF16),
        ],
        in_specs=[HBM, VMEM, VMEM],
        out_specs=[VMEM] * 3,
        scratch_shapes=[
            pltpu.VMEM((rows // tile, tile, width), BF16),
            pltpu.SemaphoreType.DMA((rows // tile,)),
        ],
        compiler_params=params(60),
        cost_estimate=pl.CostEstimate(flops=2 * rows * width * 64, bytes_accessed=2 * rows * width, transcendentals=0),
        name="column_squares",
    )(w, a_rel, b_rel)


def extras_kernel(tcb, b, sq, mag, out, buf, block_to, column_from, sems):
    fill_tables(tcb, lax.axis_index("tp"), block_to, column_from)
    scale = mag[...] * lax.rsqrt(sq[...] + 1e-06)
    row = lax.broadcasted_iota(jnp.int32, (SCALE_ROWS, BLK), 0)
    for j in range(buf.shape[0]):
        cols = slice(j * BLK, (j + 1) * BLK)
        s = scale[:, cols]
        high = s.astype(BF16).astype(F32)
        mid = (s - high).astype(BF16).astype(F32)
        low = s - high - mid
        parts = jnp.where(row == 0, high, jnp.where(row == 1, mid, jnp.where(row == 2, low, 0.0)))
        buf[j, 0:SCALE_ROWS, :] = parts.astype(BF16)
        buf[j, SCALE_ROWS:EXTRA, :] = b[:, cols]
    copies = [pltpu.make_async_copy(buf.at[block_to[r]], out.at[r], sems.at[r]) for r in range(16)]
    for c in copies:
        c.start()
    for c in copies:
        c.wait()


def pack_extras(tcb, b, sq, mag):
    per_shard = tcb.shape[1]
    return pl.pallas_call(
        extras_kernel,
        out_shape=jax.ShapeDtypeStruct((16, EXTRA, BLK), BF16),
        in_specs=[SMEM, VMEM, VMEM, VMEM],
        out_specs=HBM,
        scratch_shapes=[
            pltpu.VMEM((per_shard, EXTRA, BLK), BF16),
            pltpu.SMEM((16,), jnp.int32),
            pltpu.SMEM((16,), jnp.int32),
            pltpu.SemaphoreType.DMA((16,)),
        ],
        compiler_params=params(60),
        name="pack_extras",
    )(tcb, b, sq, mag)


def finish_kernel(blocks, first, near, tcb, a, extras, *refs):
    n = len(blocks)
    arrived, refs = refs[:n], refs[n if first else n + 1 :]
    out, raw, extra, done, block_to, column_from, raw_sems, extra_sems, done_sems = refs
    t = lax.axis_index("tp")
    fill_tables(tcb, t, block_to, column_from)
    here, fetches, stores = [], [], []
    for u, ((dx, dy), flip, at) in enumerate(blocks):
        shard = shift_to(t, (dx, (4 - dy) % 4), flip)
        column = column_from[shard]
        here.append(column >= 0)
        fetches.append([pltpu.make_async_copy(extras.at[shard], extra.at[u], extra_sems.at[u])])
        if not near:
            fetches[u].append(pltpu.make_async_copy(arrived[u].at[at], raw.at[u], raw_sems.at[u]))
        target = out.at[:, columns(jnp.maximum(column, 0))]
        stores.append(pltpu.make_async_copy(done.at[u], target, done_sems.at[u]))
    for pair in fetches:
        for c in pair:
            c.start()
    for u in range(n):
        for c in fetches[u]:
            c.wait()

        @pl.when(here[u])
        def _():
            parts = extra[u, 0:SCALE_ROWS, :].astype(F32)
            scale = parts[0:1] + parts[1:2] + parts[2:3]
            b = extra[u, SCALE_ROWS:EXTRA, :]
            block = arrived[u].at[blocks[u][2]] if near else raw.at[u]
            for lo in range(0, a.shape[0], 256):
                rows = slice(lo, lo + 256)
                low_rank = jnp.dot(a[rows, :], b, preferred_element_type=F32)
                combined = (block[rows, :].astype(F32) + low_rank).astype(BF16).astype(F32)
                done[u, rows, :] = (combined * scale).astype(BF16)
            stores[u].start()

    for u in range(n):
        pl.when(here[u])(stores[u].wait)


def finish(tcb, a, extras, blocks, merged=None, width=None, near=False):
    rows, n, first = a.shape[0], len(blocks), merged is None
    arrays = [block[2] for block in blocks] + ([] if first else [merged])
    width = width if first else merged.shape[1]
    return pl.pallas_call(
        functools.partial(finish_kernel, [(block[0], block[1], block[3]) for block in blocks], first, near),
        out_shape=jax.ShapeDtypeStruct((rows, width), BF16),
        in_specs=[SMEM, VMEM, HBM] + [VMEM if near else HBM] * n + [HBM] * (len(arrays) - n),
        out_specs=HBM,
        input_output_aliases={} if first else {3 + n: 0},
        scratch_shapes=[
            pltpu.VMEM((1 if near else n, rows, BLK), BF16),
            pltpu.VMEM((n, EXTRA, BLK), BF16),
            pltpu.VMEM((n, rows, BLK), BF16),
            pltpu.SMEM((16,), jnp.int32),
            pltpu.SMEM((16,), jnp.int32),
            pltpu.SemaphoreType.DMA((n,)),
            pltpu.SemaphoreType.DMA((n,)),
            pltpu.SemaphoreType.DMA((n,)),
        ],
        compiler_params=params(12 if near else 60),
        cost_estimate=pl.CostEstimate(
            flops=2 * n * rows * BLK * 64, bytes_accessed=4 * n * rows * BLK, transcendentals=0
        ),
        name="finish",
    )(tcb, a, extras, *arrays)


def per_device(weight, adapter_down_factor, adapter_up_factor, magnitude, training_column_block):
    tcb = training_column_block
    after = lax.optimization_barrier
    chips = ((1, 0), (0, 1), (0, 3), (1, 2))
    singles = [(o, flip) for flip in range(2) for o in ((1, 1), (1, 3), (0, 2))]
    head = list(pack(tcb, weight, [both(o) for o in chips[:3]]))
    direct = [None] * 4

    def gather(a, b, i):
        a = jnp.concatenate([a, send(a, tp_xor(A_MASKS[i]))], axis=1)
        return a, jnp.concatenate([b, send(b, fsdp_xor(B_MASKS[i]))], axis=0)

    a, b = gather(adapter_down_factor.T, adapter_up_factor, 0)
    a, b, head = after((a, b, head))
    direct[0] = send(head[0], tp_perm(chips[0]))
    a, b = after(gather(a, b, 1))
    a, b = gather(a, b, 2)
    a, head[1:3], weight_then = after((a, head[1:3], weight))
    for n in (1, 2):
        direct[n] = send(head[n], tp_perm(chips[n]))
    a = jnp.concatenate([a, send(a, tp_xor(A_MASKS[3]))], axis=1)
    sq, a, b = squares(weight, a, b)
    fourth, own = pack(tcb, weight_then, [both(chips[3]), both(OWN)])
    sq = sq + send(sq, fsdp_xor(1))
    sq, direct[:3], fourth = after((sq, direct[:3], fourth))
    direct[3] = send(fourth, tp_perm(chips[3]))
    for mask in (2, 6):
        sq = sq + send(sq, fsdp_xor(mask))
    extras = pack_extras(tcb, b, sq, magnitude[None, :])
    extras, weight_then = after((extras, weight))
    single = list(pack(tcb, weight_then, [(x,) for x in singles]))
    extras = lax.all_to_all(extras, "tp", split_axis=0, concat_axis=0, tiled=True)
    extras, direct[3], single, own = after((extras, direct[3], single, own))
    single = [send(m, tp_perm(*x)) for m, x in zip(single, singles)]
    blocks = [(OWN, 0, own, 0), (OWN, 1, send(own, tp_xor(1)), 1)]
    for o, m in zip(chips, direct):
        blocks += [(o, 0, m, 0), (o, 1, send(m, tp_xor(1)), 1)]
    blocks += [(*x, m, 0) for x, m in zip(singles, single)]
    merged = finish(tcb, a, extras, blocks[:10], width=weight.shape[1])
    merged = finish(tcb, a, extras, blocks[10:13], merged)
    return finish(tcb, a, extras, blocks[13:], merged, near=True)


def solution(mesh):
    return jax.shard_map(
        per_device,
        mesh=mesh,
        in_specs=(P("fsdp", "tp"), P(("fsdp", "tp"), None), P("fsdp", "tp"), P("tp"), P()),
        out_specs=P("fsdp", "tp"),
        check_vma=False,
    )
```

```python
import functools

import jax
import jax.numpy as jnp
from jax import lax
from jax.experimental import pallas as pl
from jax.experimental.pallas import tpu as pltpu
from jax.sharding import PartitionSpec as P

AXES = ("fsdp", "tp")
BLK = 128
SCALE_ROWS = 16
EXTRA = 80
OWN = (0, 0)
A_MASKS = (8, 2, 6, 1)
B_MASKS = (1, 2, 6)
BF16, F32 = jnp.bfloat16, jnp.float32
HBM = pl.BlockSpec(memory_space=pltpu.HBM)
ANY = pl.BlockSpec(memory_space=pl.ANY)
SMEM = pl.BlockSpec(memory_space=pltpu.SMEM)
VMEM = pl.BlockSpec(memory_space=pltpu.VMEM)


def shift_to(t, offset, flip):
    hi, y, core = t // 8, (t // 2) % 4, t % 2
    return ((hi + offset[0]) % 2) * 8 + ((y + offset[1]) % 4) * 2 + (core + flip) % 2


def tp_perm(offset, flip=0):
    return [(f * 16 + t, f * 16 + shift_to(t, offset, flip)) for f in range(8) for t in range(16)]


def tp_xor(mask):
    return [(f * 16 + t, f * 16 + (t ^ mask)) for f in range(8) for t in range(16)]


def fsdp_xor(mask):
    return [(f * 16 + t, (f ^ mask) * 16 + t) for f in range(8) for t in range(16)]


def send(x, perm):
    return lax.ppermute(x, AXES, perm)


def fill_tables(tcb, t, block_to, column_from):
    for i in range(16):
        block_to[i] = 0
        column_from[i] = -1
    for s in range(tcb.shape[1]):
        value = tcb[0, s]
        shard = value // tcb.shape[1]
        shift = (16 - shard) % 16
        block_to[(t + shift) % 16] = value - shard * tcb.shape[1]
        column_from[(t + 16 - shift) % 16] = s


def params(limit_mib, **kw):
    return pltpu.CompilerParams(vmem_limit_bytes=limit_mib << 20, **kw)


def columns(j):
    return pl.ds(pl.multiple_of(j * BLK, BLK), BLK)


def both(offset):
    return ((offset, 0), (offset, 1))


def pack_kernel(messages, tcb, w, *refs):
    outs, (buf, block_to, column_from, in_sems, out_sems) = refs[: len(messages)], refs[len(messages) :]
    t = lax.axis_index("tp")
    fill_tables(tcb, t, block_to, column_from)
    copies = []
    for out, message in zip(outs, messages):
        for n, (offset, flip) in enumerate(message):
            i, j = len(copies), block_to[shift_to(t, offset, flip)]
            copies.append(
                (
                    pltpu.make_async_copy(w.at[:, columns(j)], buf.at[i], in_sems.at[i]),
                    pltpu.make_async_copy(buf.at[i], out.at[n], out_sems.at[i]),
                )
            )
    for fetch, _ in copies:
        fetch.start()
    for fetch, store in copies:
        fetch.wait()
        store.start()
    for _, store in copies:
        store.wait()


def pack(tcb, w, messages):
    rows, count = w.shape[0], sum(len(m) for m in messages)
    return pl.pallas_call(
        functools.partial(pack_kernel, messages),
        out_shape=[jax.ShapeDtypeStruct((len(m), rows, BLK), BF16) for m in messages],
        in_specs=[SMEM, HBM],
        out_specs=[HBM] * len(messages),
        scratch_shapes=[
            pltpu.VMEM((count, rows, BLK), BF16),
            pltpu.SMEM((16,), jnp.int32),
            pltpu.SMEM((16,), jnp.int32),
            pltpu.SemaphoreType.DMA((count,)),
            pltpu.SemaphoreType.DMA((count,)),
        ],
        compiler_params=params(60),
        cost_estimate=pl.CostEstimate(flops=0, bytes_accessed=count * 4 * rows * BLK, transcendentals=0),
        name="pack",
    )(tcb, w)


def squares_kernel(w_hbm, a_rel, b_rel, sq, a_ord, b_ord, w, sems):
    t, f = lax.axis_index("tp"), lax.axis_index("fsdp")
    count, tile, width = w.shape
    fetches = [
        pltpu.make_async_copy(w_hbm.at[pl.ds(i * tile, tile)], w.at[i], sems.at[i]) for i in range(count)
    ]
    for c in fetches:
        c.start()
    row = lax.broadcasted_iota(jnp.int32, (64, 64), 0)
    col = lax.broadcasted_iota(jnp.int32, (64, 64), 1)
    slot = col >> 3
    shard = (slot ^ ((slot >> 1) & 2)) ^ f
    place = jnp.where(row == shard * 8 + (col & 7), 1.0, 0.0).astype(BF16)
    b_ord[...] = jnp.dot(place, b_rel[...], preferred_element_type=F32).astype(BF16)
    for i in range(16):
        rel = i ^ t
        r0, r1, r2, r3 = rel & 1, (rel >> 1) & 1, (rel >> 2) & 1, (rel >> 3) & 1
        slot = r3 | ((r1 ^ r2) << 1) | (r2 << 2) | (r0 << 3)
        a_ord[i * 128 : (i + 1) * 128, :] = a_rel[:, columns(slot)].astype(F32).T.astype(BF16)
    sums = [jnp.zeros((8, min(256, width - lo)), F32) for lo in range(0, width, 256)]
    for i in range(count):
        fetches[i].wait()
        a = a_ord[i * tile : (i + 1) * tile, :]
        for n, lo in enumerate(range(0, width, 256)):
            hi = min(lo + 256, width)
            low_rank = jnp.dot(a, b_ord[:, lo:hi], preferred_element_type=F32)
            combined = (w[i, :, lo:hi].astype(F32) + low_rank).astype(BF16).astype(F32)
            sums[n] += jnp.sum((combined * combined).reshape(tile // 8, 8, hi - lo), axis=0)
    for n, lo in enumerate(range(0, width, 256)):
        sq[:, lo : min(lo + 256, width)] = jnp.sum(sums[n], axis=0, keepdims=True)


def squares(w, a_rel, b_rel, tile=256):
    rows, width = w.shape
    return pl.pallas_call(
        squares_kernel,
        out_shape=[
            jax.ShapeDtypeStruct((1, width), F32),
            jax.ShapeDtypeStruct((rows, 64), BF16),
            jax.ShapeDtypeStruct((64, width), BF16),
        ],
        in_specs=[HBM, VMEM, VMEM],
        out_specs=[VMEM] * 3,
        scratch_shapes=[
            pltpu.VMEM((rows // tile, tile, width), BF16),
            pltpu.SemaphoreType.DMA((rows // tile,)),
        ],
        compiler_params=params(60),
        cost_estimate=pl.CostEstimate(flops=2 * rows * width * 64, bytes_accessed=2 * rows * width, transcendentals=0),
        name="column_squares",
    )(w, a_rel, b_rel)


def extras_kernel(tcb, b, sq, mag, out, buf, block_to, column_from, sems):
    fill_tables(tcb, lax.axis_index("tp"), block_to, column_from)
    scale = mag[...] * lax.rsqrt(sq[...] + 1e-06)
    row = lax.broadcasted_iota(jnp.int32, (SCALE_ROWS, BLK), 0)
    for j in range(buf.shape[0]):
        cols = slice(j * BLK, (j + 1) * BLK)
        s = scale[:, cols]
        high = s.astype(BF16).astype(F32)
        mid = (s - high).astype(BF16).astype(F32)
        low = s - high - mid
        parts = jnp.where(row == 0, high, jnp.where(row == 1, mid, jnp.where(row == 2, low, 0.0)))
        buf[j, 0:SCALE_ROWS, :] = parts.astype(BF16)
        buf[j, SCALE_ROWS:EXTRA, :] = b[:, cols]
    copies = [pltpu.make_async_copy(buf.at[block_to[r]], out.at[r], sems.at[r]) for r in range(16)]
    for c in copies:
        c.start()
    for c in copies:
        c.wait()


def pack_extras(tcb, b, sq, mag):
    per_shard = tcb.shape[1]
    return pl.pallas_call(
        extras_kernel,
        out_shape=jax.ShapeDtypeStruct((16, EXTRA, BLK), BF16),
        in_specs=[SMEM, VMEM, VMEM, VMEM],
        out_specs=HBM,
        scratch_shapes=[
            pltpu.VMEM((per_shard, EXTRA, BLK), BF16),
            pltpu.SMEM((16,), jnp.int32),
            pltpu.SMEM((16,), jnp.int32),
            pltpu.SemaphoreType.DMA((16,)),
        ],
        compiler_params=params(60),
        name="pack_extras",
    )(tcb, b, sq, mag)


def finish_kernel(blocks, first, near, tcb, a, extras, *refs):
    n = len(blocks)
    arrived, refs = refs[:n], refs[n if first else n + 1 :]
    out, raw, extra, done, block_to, column_from, raw_sems, extra_sems, done_sems = refs
    t = lax.axis_index("tp")
    fill_tables(tcb, t, block_to, column_from)
    here, fetches, stores = [], [], []
    for u, ((dx, dy), flip, at) in enumerate(blocks):
        shard = shift_to(t, (dx, (4 - dy) % 4), flip)
        column = column_from[shard]
        here.append(column >= 0)
        fetches.append([pltpu.make_async_copy(extras.at[shard], extra.at[u], extra_sems.at[u])])
        if not near:
            fetches[u].append(pltpu.make_async_copy(arrived[u].at[at], raw.at[u], raw_sems.at[u]))
        target = out.at[:, columns(jnp.maximum(column, 0))]
        stores.append(pltpu.make_async_copy(done.at[u], target, done_sems.at[u]))
    for pair in fetches:
        for c in pair:
            c.start()
    for u in range(n):
        for c in fetches[u]:
            c.wait()

        @pl.when(here[u])
        def _():
            parts = extra[u, 0:SCALE_ROWS, :].astype(F32)
            scale = parts[0:1] + parts[1:2] + parts[2:3]
            b = extra[u, SCALE_ROWS:EXTRA, :]
            block = arrived[u].at[blocks[u][2]] if near else raw.at[u]
            for lo in range(0, a.shape[0], 256):
                rows = slice(lo, lo + 256)
                low_rank = jnp.dot(a[rows, :], b, preferred_element_type=F32)
                combined = (block[rows, :].astype(F32) + low_rank).astype(BF16).astype(F32)
                done[u, rows, :] = (combined * scale).astype(BF16)
            stores[u].start()

    for u in range(n):
        pl.when(here[u])(stores[u].wait)


def finish(tcb, a, extras, blocks, merged=None, width=None, near=False):
    rows, n, first = a.shape[0], len(blocks), merged is None
    arrays = [block[2] for block in blocks] + ([] if first else [merged])
    width = width if first else merged.shape[1]
    return pl.pallas_call(
        functools.partial(finish_kernel, [(block[0], block[1], block[3]) for block in blocks], first, near),
        out_shape=jax.ShapeDtypeStruct((rows, width), BF16),
        in_specs=[SMEM, VMEM, HBM] + [VMEM if near else HBM] * n + [HBM] * (len(arrays) - n),
        out_specs=HBM,
        input_output_aliases={} if first else {3 + n: 0},
        scratch_shapes=[
            pltpu.VMEM((1 if near else n, rows, BLK), BF16),
            pltpu.VMEM((n, EXTRA, BLK), BF16),
            pltpu.VMEM((n, rows, BLK), BF16),
            pltpu.SMEM((16,), jnp.int32),
            pltpu.SMEM((16,), jnp.int32),
            pltpu.SemaphoreType.DMA((n,)),
            pltpu.SemaphoreType.DMA((n,)),
            pltpu.SemaphoreType.DMA((n,)),
        ],
        compiler_params=params(12 if near else 60),
        cost_estimate=pl.CostEstimate(
            flops=2 * n * rows * BLK * 64, bytes_accessed=4 * n * rows * BLK, transcendentals=0
        ),
        name="finish",
    )(tcb, a, extras, *arrays)


def per_device(weight, adapter_down_factor, adapter_up_factor, magnitude, training_column_block):
    tcb = training_column_block
    after = lax.optimization_barrier
    chips = ((1, 0), (0, 1), (0, 3), (1, 2))
    singles = [(o, flip) for flip in range(2) for o in ((1, 1), (1, 3), (0, 2))]
    head = list(pack(tcb, weight, [both(o) for o in chips[:3]]))
    direct = [None] * 4

    def gather(a, b, i):
        a = jnp.concatenate([a, send(a, tp_xor(A_MASKS[i]))], axis=1)
        return a, jnp.concatenate([b, send(b, fsdp_xor(B_MASKS[i]))], axis=0)

    a, b = gather(adapter_down_factor.T, adapter_up_factor, 0)
    a, b, head = after((a, b, head))
    direct[0] = send(head[0], tp_perm(chips[0]))
    a, b = gather(a, b, 1)
    a = jnp.concatenate([a, send(a, tp_xor(A_MASKS[2]))], axis=1)
    a, b, head[1:3], weight_then = after((a, b, head[1:3], weight))
    b = jnp.concatenate([b, send(b, fsdp_xor(B_MASKS[2]))], axis=0)
    for n in (1, 2):
        direct[n] = send(head[n], tp_perm(chips[n]))
    a = jnp.concatenate([a, send(a, tp_xor(A_MASKS[3]))], axis=1)
    sq, a, b = squares(weight, a, b)
    fourth, own = pack(tcb, weight_then, [both(chips[3]), both(OWN)])
    sq = sq + send(sq, fsdp_xor(1))
    sq, direct[:3], fourth = after((sq, direct[:3], fourth))
    direct[3] = send(fourth, tp_perm(chips[3]))
    for mask in (2, 6):
        sq = sq + send(sq, fsdp_xor(mask))
    extras = pack_extras(tcb, b, sq, magnitude[None, :])
    extras, weight_then = after((extras, weight))
    single = list(pack(tcb, weight_then, [(x,) for x in singles]))
    extras = lax.all_to_all(extras, "tp", split_axis=0, concat_axis=0, tiled=True)
    extras, direct[3], single, own = after((extras, direct[3], single, own))
    single = [send(m, tp_perm(*x)) for m, x in zip(single, singles)]
    blocks = [(OWN, 0, own, 0), (OWN, 1, send(own, tp_xor(1)), 1)]
    for o, m in zip(chips, direct):
        blocks += [(o, 0, m, 0), (o, 1, send(m, tp_xor(1)), 1)]
    blocks += [(*x, m, 0) for x, m in zip(singles, single)]
    merged = finish(tcb, a, extras, blocks[:10], width=weight.shape[1])
    merged = finish(tcb, a, extras, blocks[10:13], merged)
    return finish(tcb, a, extras, blocks[13:], merged, near=True)


def solution(mesh):
    return jax.shard_map(
        per_device,
        mesh=mesh,
        in_specs=(P("fsdp", "tp"), P(("fsdp", "tp"), None), P("fsdp", "tp"), P("tp"), P()),
        out_specs=P("fsdp", "tp"),
        check_vma=False,
    )
```
